32 devices in a mesh: span: 8 (over z, x), sp: 2 (over y), fsdp: 2 (over core).
Axes of the slice: x: 2, y: 2, z: 4, core: 2. Of those that a mesh axis runs over, the one named last changes fastest.
Arguments:
- query_pre: bfloat16 [2, 2048, 3072], P('fsdp', ('span', 'sp')), may hold values from -12 to 12
- key_pre: bfloat16 [2, 2048, 3072], P('fsdp', ('span', 'sp')), may hold values from -12 to 12
- values: bfloat16 [2, 2048, 3072], P('fsdp', ('span', 'sp')), may hold values from -6 to 6
- cotangent: bfloat16 [2, 2048, 3072], P('fsdp', ('span', 'sp')), may hold values from -6 to 6
- gains: float32 [2, 3072], P(None, 'fsdp'), may hold values from 0.5 to 1.5
- frame_span: int32 [2, 2048], P('fsdp', 'span'), may hold values from 0 to 15, as said below
- denoise_steps: int32 [2, 16], P('fsdp'), may hold values from 1 to 4
Outputs:
- query_grad: bfloat16 [2, 2048, 3072], P('fsdp', ('span', 'sp'))
- key_grad: bfloat16 [2, 2048, 3072], P('fsdp', ('span', 'sp'))
- value_grad: bfloat16 [2, 2048, 3072], P('fsdp', ('span', 'sp'))
- gain_grad: float32 [2, 3072], P(None, 'fsdp')
The draws below stay inside these ranges and needn't reach their ends.
Inputs may be any that keep to these rules, and one draw needn't show every extreme that they name: `frame_span`: never falls along a video. Group g (tokens g * 256 to (g + 1) * 256 - 1) holds frame spans 2 g and 2 g + 1, each from a quarter to three quarters of the group's tokens.
All inputs are finite; a program needn't handle non-finite values.
Results may differ from the reference program's by a relative error of at most 0.0081.
The reference program's roundings to bfloat16 on the way count: a program that leaves them out, or rounds other values in their place, can miss the bound.
Values may be sent and summed in bfloat16 or wider, within the bound.
A program may use at most 128 MiB of HBM per device.

```python
import jax
import jax.numpy as jnp
from jax import lax

TOK_DEV = 128
HEADS = 24
HDIM = 128
CHANNELS = 3072
TOKENS = 2048
SPANS = 16
VIDEOS = 2
N_SPAN = 8
N_SP = 2


def draw_frame_span(key, part):
    block = TOK_DEV * N_SP
    bounds = jax.random.randint(key, (VIDEOS, N_SPAN), block // 4, 3 * block // 4 + 1)
    positions = jnp.arange(block, dtype=jnp.int32)
    later = (positions[None, None, :] >= bounds[:, :, None]).astype(jnp.int32)
    base = 2 * jnp.arange(N_SPAN, dtype=jnp.int32)
    return (base[None, :, None] + later).reshape(VIDEOS, TOKENS).astype(jnp.int32)


def drawn_rows(key, salt):
    third = jax.random.fold_in(jax.random.fold_in(key, salt), 2)
    return jnp.clip(jax.random.normal(third, (VIDEOS, TOKENS, CHANNELS), jnp.float32), -6.0, 6.0)


def draw_query_pre(key, part):
    rows = drawn_rows(key, 11)
    return rows.astype(jnp.bfloat16)


def draw_key_pre(key, part):
    rows = drawn_rows(key, 12)
    return rows.astype(jnp.bfloat16)


def touch_ends(values, stream_key, low, largest):
    longest = values.shape.index(max(values.shape))
    spots = []
    for shift in (0, 1):
        where = [jax.random.randint(jax.random.fold_in(stream_key, axis), (), 0, length) for axis, length in enumerate(values.shape)]
        where[longest] = (where[longest] + shift) % values.shape[longest]
        spots.append(tuple(where))
    return values.at[spots[0]].set(low).at[spots[1]].set(largest)


def block_levels(key, shape, cuts, least, top_value):
    loudness = 1.0
    for dim, blocks in cuts:
        draws = jax.random.uniform(jax.random.fold_in(jax.random.fold_in(key, 6), dim), (blocks,), jnp.float32, least / len(cuts), top_value / len(cuts))
        loudness = loudness * jnp.repeat(jnp.exp(draws), shape[dim] // blocks).reshape((-1,) + (1,) * (len(shape) - 1 - dim))
    return loudness


def centred(rng, shape, deviation, most, cuts=(), kind=jnp.bfloat16):
    array = deviation * jax.random.normal(rng, shape, jnp.float32)
    if cuts:
        array = array * block_levels(rng, shape, cuts, -0.22, 0.18)
    return jnp.clip(array, -most, most).astype(kind)


def setup_inputs(seed: int = 0) -> dict:
    key_list = jax.random.split(jax.random.key(seed), 8)
    return {
        "query_pre": draw_query_pre(jax.random.fold_in(key_list[7], 71), 0),
        "key_pre": draw_key_pre(jax.random.fold_in(key_list[7], 71), 0),
        "values": centred(key_list[2], (VIDEOS, TOKENS, CHANNELS), 1.0, 6.0, ((0, 2), (1, 16))),
        "cotangent": centred(key_list[3], (VIDEOS, TOKENS, CHANNELS), 1.0, 6.0, ((0, 2), (1, 16))),
        "gains": jnp.clip(1.0 + 0.1 * jax.random.normal(key_list[4], (2, CHANNELS), jnp.float32), 0.5, 1.5),
        "frame_span": draw_frame_span(jax.random.fold_in(key_list[7], 71), 0),
        "denoise_steps": touch_ends(jax.random.randint(key_list[6], (VIDEOS, SPANS), 1, 5), jax.random.fold_in(key_list[6], 1), 1, 4).astype(jnp.int32),
    }


EPSILON = 1e-06
NEGATIVE = -1e+30

def normed(raw_rows, gain_row):
    wide = raw_rows.astype(jnp.float32)
    inverse_rms = lax.rsqrt(lax.optimization_barrier(jnp.mean(wide * wide, axis=-1, keepdims=True)) + EPSILON)
    normal_rows = wide * inverse_rms
    return (normal_rows, inverse_rms, (normal_rows * gain_row).astype(jnp.bfloat16))

def norm_backward(grad_rows, normal_rows, inverse_rms, gain_row):
    upstream = grad_rows.astype(jnp.float32)
    scaled = upstream * gain_row
    inner = lax.optimization_barrier(jnp.mean(scaled * normal_rows, axis=-1, keepdims=True))
    result = (inverse_rms * (scaled - normal_rows * inner)).astype(jnp.bfloat16)
    return (result, lax.optimization_barrier(jnp.sum(upstream * normal_rows, axis=0)))

def across(left, right):
    return lax.dot_general(left, right, (((1,), (1,)), ((), ())), preferred_element_type=jnp.float32)

def downward(left, right):
    return lax.dot_general(left, right, (((0,), (0,)), ((), ())), preferred_element_type=jnp.float32)

def head_grads(query_head, grad_head, key_own, value_own, key_prev, value_prev, own_mask, prev_open, step_weight):
    score_scale = HDIM ** (-0.5)
    score_own = across(query_head, key_own) * score_scale
    score_prev = across(query_head, key_prev) * score_scale
    masked_own = jnp.where(own_mask, score_own, NEGATIVE)
    masked_prev = jnp.where(prev_open, score_prev, NEGATIVE)
    row_max = jnp.maximum(lax.optimization_barrier(jnp.max(masked_own, axis=1)), lax.optimization_barrier(jnp.max(masked_prev, axis=1)))
    row_total = lax.optimization_barrier(jnp.sum(jnp.exp(masked_own - row_max[:, None]), axis=1)) + lax.optimization_barrier(jnp.sum(jnp.exp(masked_prev - row_max[:, None]), axis=1))
    log_total = row_max + jnp.log(row_total)
    prob_own = jnp.where(own_mask, jnp.exp(score_own - log_total[:, None]), 0.0)
    prob_prev = jnp.where(prev_open, jnp.exp(score_prev - log_total[:, None]), 0.0)
    grad_prob_own = across(grad_head, value_own)
    grad_prob_prev = across(grad_head, value_prev)
    row_delta = lax.optimization_barrier(jnp.sum(prob_own * grad_prob_own, axis=1)) + lax.optimization_barrier(jnp.sum(prob_prev * grad_prob_prev, axis=1))
    factor = step_weight[:, None]
    sgrad_own = (factor * prob_own * (grad_prob_own - row_delta[:, None])).astype(jnp.bfloat16)
    sgrad_prev = (factor * prob_prev * (grad_prob_prev - row_delta[:, None])).astype(jnp.bfloat16)
    weight_own = (factor * prob_own).astype(jnp.bfloat16)
    weight_prev = (factor * prob_prev).astype(jnp.bfloat16)
    query_part = (jnp.dot(sgrad_own, key_own, preferred_element_type=jnp.float32) + jnp.dot(sgrad_prev, key_prev, preferred_element_type=jnp.float32)) * score_scale
    key_own_grad = downward(sgrad_own, query_head) * score_scale
    value_own_grad = downward(weight_own, grad_head)
    key_prev_grad = downward(sgrad_prev, query_head) * score_scale
    value_prev_grad = downward(weight_prev, grad_head)
    return (query_part, key_own_grad, value_own_grad, key_prev_grad, value_prev_grad)

def reference(query_pre, key_pre, values, cotangent, gains, frame_span, denoise_steps):
    block = TOK_DEV * N_SP
    gain_total = jnp.zeros((2, HEADS * HDIM), jnp.float32)
    query_outs = []
    key_outs = []
    value_outs = []

    def split_heads(rows):
        return rows.reshape(N_SPAN, block, HEADS, HDIM).transpose(0, 2, 1, 3)

    def join_heads(parts):
        return parts.transpose(0, 2, 1, 3).reshape(N_SPAN * block, HEADS * HDIM)
    for video in range(VIDEOS):
        q_normal, q_inverse, q_ready = normed(query_pre[video], gains[0])
        k_normal, k_inverse, k_ready = normed(key_pre[video], gains[1])
        span_ids = frame_span[video]
        step_weight = denoise_steps[video][span_ids].astype(jnp.float32)
        query_heads = split_heads(q_ready)
        key_heads = split_heads(k_ready)
        value_heads = split_heads(values[video])
        grad_heads = split_heads(cotangent[video])
        results = []
        for group_index in range(N_SPAN):
            earlier = max(group_index - 1, 0)
            ids_here = span_ids[group_index * block:(group_index + 1) * block]
            own_mask = ids_here[None, :] <= ids_here[:, None]
            weight_here = step_weight[group_index * block:(group_index + 1) * block]
            prev_open = group_index > 0

            def one_head(operands, own_mask=own_mask, prev_open=prev_open, weight_here=weight_here):
                query_head, grad_head, key_own, value_own, key_prev, value_prev = operands
                return head_grads(query_head, grad_head, key_own, value_own, key_prev, value_prev, own_mask, prev_open, weight_here)
            results.append(lax.map(one_head, (query_heads[group_index], grad_heads[group_index], key_heads[group_index], value_heads[group_index], key_heads[earlier], value_heads[earlier])))
        query_parts = []
        key_parts = []
        value_parts = []
        for group_index in range(N_SPAN):
            key_sum = results[group_index][1]
            value_sum = results[group_index][2]
            if group_index + 1 < N_SPAN:
                key_sum = key_sum + results[group_index + 1][3]
                value_sum = value_sum + results[group_index + 1][4]
            query_parts.append(results[group_index][0].astype(jnp.bfloat16))
            key_parts.append(key_sum.astype(jnp.bfloat16))
            value_parts.append(value_sum.astype(jnp.bfloat16))
        query_attn = join_heads(jnp.stack(query_parts))
        key_attn = join_heads(jnp.stack(key_parts))
        value_attn = join_heads(jnp.stack(value_parts))
        query_back, query_gain = norm_backward(query_attn, q_normal, q_inverse, gains[0])
        key_back, key_gain = norm_backward(key_attn, k_normal, k_inverse, gains[1])
        gain_total = gain_total + jnp.stack([query_gain, key_gain])
        query_outs.append(query_back)
        key_outs.append(key_back)
        value_outs.append(value_attn)
    return (jnp.stack(query_outs), jnp.stack(key_outs), jnp.stack(value_outs), gain_total)
```

```python
import functools
import math

import jax
import jax.numpy as jnp
from jax import lax
from jax.experimental import pallas as pl
from jax.experimental.pallas import tpu as pltpu
from jax.sharding import PartitionSpec as P

HDIM = 128
EPSILON = 1e-06
NEGATIVE = -1e30
F32 = jnp.float32
BF16 = jnp.bfloat16
ROWS = 16


def dot(left, right, left_dim, right_dim):
    return lax.dot_general(
        left, right, (((left_dim,), (right_dim,)), ((), ())), preferred_element_type=F32
    )


def kernel(
    sizes,
    query_ref, key_ref, value_ref, grad_ref, gain_ref, span_ref, steps_ref,
    query_out, key_out, value_out, gain_out,
    gain_full, q_ready, k_ready, q_inverse, k_inverse,
    heads_query, heads_grad, key_joined, value_joined, bias, weight_row,
    own_key, own_value, send_key, send_value, back_key, back_value,
    dq_heads, dk_heads, dv_heads, dq_rows, dk_rows, dv_rows,
    gain_part, gain_rows, pair_recv, tree_send, tree_recv,
    gain_s, gain_r, in_s, in_r, in_local, ahead_s, ahead_r, behind_s, behind_r,
    out_s, out_r, out_local, pair_s, pair_r, tree_s, tree_r,
):
    n_span, n_sp, n_fsdp, chunks, per_chunk = sizes
    tokens, channels = q_ready.shape
    group, width = heads_query.shape
    part = channels // n_fsdp
    chunk_width = per_chunk * HDIM
    query_block = math.gcd(group, 256)
    scale = HDIM ** (-0.5)
    g, s, f = lax.axis_index("span"), lax.axis_index("sp"), lax.axis_index("fsdp")
    after, before = lax.rem(g + 1, n_span), lax.rem(g + n_span - 1, n_span)
    has_before, has_after = g > 0, g < n_span - 1

    def partner(index, step):
        return index + step * (1 - 2 * lax.rem(index // step, 2))

    sp_steps = [1 << b for b in range(n_sp.bit_length() - 1)]
    span_steps = [1 << b for b in range(n_span.bit_length() - 1)]
    tree = [("sp", partner(s, step)) for step in sp_steps]
    tree += [("span", partner(g, step)) for step in span_steps]

    barrier = pltpu.get_barrier_semaphore()

    def greet(device):
        pl.semaphore_signal(
            barrier, inc=1, device_id=device, device_id_type=pl.DeviceIdType.MESH
        )

    count = 0
    for d in range(1, n_fsdp):
        greet({"fsdp": lax.rem(f + d, n_fsdp)})
        count += 1
    for d in range(1, n_sp):
        greet({"sp": lax.rem(s + d, n_sp)})
        count += 1
    for step in span_steps[1:]:
        greet({"span": partner(g, step)})
        count += 1

    @pl.when(has_before)
    def _():
        greet({"span": before})

    @pl.when(has_after)
    def _():
        greet({"span": after})

    count += lax.div(g + n_span - 1, n_span) + lax.div(2 * n_span - 2 - g, n_span)
    pl.semaphore_wait(barrier, count)

    def remote(src, dst, send, recv, device):
        return pltpu.make_async_remote_copy(
            src_ref=src, dst_ref=dst, send_sem=send, recv_sem=recv,
            device_id=device, device_id_type=pl.DeviceIdType.MESH,
        )

    def columns(c):
        return pl.ds(pl.multiple_of(c * chunk_width, HDIM), chunk_width)

    def shifted(base, c):
        return pl.ds(pl.multiple_of(base * width + c * chunk_width, HDIM), chunk_width)

    def row_block(index):
        return pl.ds(pl.multiple_of(index * tokens, tokens), tokens)

    sources = (k_ready, value_ref.at[0], q_ready, grad_ref.at[0])
    homes = (key_joined, value_joined, heads_query, heads_grad)

    def incoming(a, c, d):
        peer = lax.rem(s + d, n_sp)
        return remote(
            sources[a].at[:, shifted(peer, c)], homes[a].at[row_block(s), columns(c)],
            in_s.at[a, c, d - 1], in_r.at[a, c, d - 1], {"sp": peer},
        )

    def incoming_local(a):
        return pltpu.make_async_copy(
            sources[a].at[:, pl.ds(pl.multiple_of(s * width, HDIM), width)],
            homes[a].at[row_block(s), :], in_local.at[a],
        )

    def ahead(a, c):
        home = homes[a]
        return remote(
            home.at[pl.ds(0, group), columns(c)], home.at[pl.ds(group, group), columns(c)],
            ahead_s.at[a, c], ahead_r.at[a, c], {"span": after},
        )

    def behind(a, c):
        return remote(
            (send_key, send_value)[a].at[:, columns(c)],
            (back_key, back_value)[a].at[:, columns(c)],
            behind_s.at[a, c], behind_r.at[a, c], {"span": before},
        )

    results = (dq_heads, dk_heads, dv_heads)
    landed = (dq_rows, dk_rows, dv_rows)

    def outgoing(a, c, d):
        peer = lax.rem(s + d, n_sp)
        return remote(
            results[a].at[row_block(peer), columns(c)], landed[a].at[:, shifted(s, c)],
            out_s.at[a, c, d - 1], out_r.at[a, c, d - 1], {"sp": peer},
        )

    def outgoing_local(a, c):
        return pltpu.make_async_copy(
            results[a].at[row_block(s), columns(c)], landed[a].at[:, shifted(s, c)],
            out_local.at[a, c],
        )

    def gain_copy(d):
        mine = pl.ds(pl.multiple_of(f * part, HDIM), part)
        return remote(
            gain_ref, gain_full.at[:, mine], gain_s.at[d - 1], gain_r.at[d - 1],
            {"fsdp": lax.rem(f + d, n_fsdp)},
        )

    peers = range(1, n_sp)
    for d in range(1, n_fsdp):
        gain_copy(d).start()
    for a in (1, 3):
        for d in peers:
            incoming(a, 0, d).start()
        incoming_local(a).start()
    gain_full[:, pl.ds(pl.multiple_of(f * part, HDIM), part)] = gain_ref[...]

    @pl.when(g == 0)
    def _():
        key_joined[group:, :] = jnp.zeros((group, width), BF16)
        value_joined[group:, :] = jnp.zeros((group, width), BF16)

    @pl.when(g == n_span - 1)
    def _():
        back_key[...] = jnp.zeros_like(back_key)
        back_value[...] = jnp.zeros_like(back_value)

    for d in range(1, n_fsdp):
        gain_copy(d).wait_recv()

    def norm(raw_ref, row, inverse_ref, ready_ref):
        def block(i, carry):
            rows = pl.ds(pl.multiple_of(i * ROWS, ROWS), ROWS)
            wide = raw_ref[0, rows, :].astype(F32)
            inverse = lax.rsqrt(
                jnp.sum(wide * wide, axis=1, keepdims=True) * (1.0 / channels) + EPSILON
            )
            inverse_ref[rows, :] = inverse
            ready_ref[rows, :] = (wide * inverse * gain_full[row : row + 1, :]).astype(BF16)
            return carry

        lax.fori_loop(0, tokens // ROWS, block, 0)

    norm(key_ref, 1, k_inverse, k_ready)
    for d in peers:
        incoming(0, 0, d).start()
    incoming_local(0).start()
    norm(query_ref, 0, q_inverse, q_ready)
    for d in peers:
        incoming(2, 0, d).start()
    incoming_local(2).start()

    def start_chunk(c, carry):
        for a in range(4):
            for d in peers:
                incoming(a, c, d).start()
        return carry

    lax.fori_loop(1, chunks, start_chunk, 0)

    ids = span_ref[...]
    ids_down = jnp.transpose(jnp.broadcast_to(ids.astype(F32), (HDIM, group)))[:, :1]
    bias[:group, :] = jnp.where(ids_down <= ids.astype(F32), 0.0, NEGATIVE)
    bias[group:, :] = jnp.zeros((group, group), F32) + jnp.where(has_before, 0.0, NEGATIVE)
    weight = jnp.zeros(ids.shape, F32)
    for index in range(steps_ref.shape[1]):
        weight = jnp.where(ids == index, steps_ref[0, index].astype(F32), weight)
    weight_row[...] = weight

    for a in range(4):
        incoming_local(a).wait()

    def forward(c):
        for a in (0, 1):
            for d in peers:
                incoming(a, c, d).wait_recv()

            @pl.when(has_after)
            def _():
                ahead(a, c).start()

    def one_block(head, block_index):
        cols = pl.ds(pl.multiple_of(head * HDIM, HDIM), HDIM)
        if query_block == group:
            rows = pl.ds(0, group)
        else:
            rows = pl.ds(pl.multiple_of(block_index * query_block, query_block), query_block)
        query = heads_query[rows, cols]
        grad = heads_grad[rows, cols]
        keys = key_joined[:, cols]
        scores = dot(keys, query, 1, 1) * (scale * math.log2(math.e)) + bias[:, rows]
        top = jnp.max(scores, axis=0, keepdims=True)
        raised = jnp.exp2(scores - top)
        inverse_total = 1.0 / jnp.sum(raised, axis=0, keepdims=True)
        grad_prob = dot(value_joined[:, cols], grad, 1, 1)
        delta = jnp.sum(raised * grad_prob, axis=0, keepdims=True) * inverse_total
        weighted = raised * (weight_row[:, rows] * inverse_total)
        sgrad = (weighted * (grad_prob - delta)).astype(BF16)
        weights = weighted.astype(BF16)
        dq_heads[rows, cols] = (dot(sgrad, keys, 0, 0) * scale).astype(BF16)
        return dot(sgrad, query, 1, 0) * scale, dot(weights, grad, 1, 0)

    def one_head(head):
        cols = pl.ds(pl.multiple_of(head * HDIM, HDIM), HDIM)
        if query_block == group:
            key_term, value_term = one_block(head, 0)
        else:
            zero = jnp.zeros((2 * group, HDIM), F32)

            def add(i, total):
                terms = one_block(head, i)
                return total[0] + terms[0], total[1] + terms[1]

            key_term, value_term = lax.fori_loop(0, group // query_block, add, (zero, zero))
        own_key[:, cols] = key_term[:group]
        own_value[:, cols] = value_term[:group]
        send_key[:, cols] = key_term[group:].astype(BF16)
        send_value[:, cols] = value_term[group:].astype(BF16)

    def compute(c):
        for a in (2, 3):
            for d in peers:
                incoming(a, c, d).wait_recv()

        @pl.when(has_before)
        def _():
            for a in (0, 1):
                ahead(a, c).wait_recv()

        def head_step(i, carry):
            one_head(c * per_chunk + i)
            return carry

        lax.fori_loop(0, per_chunk, head_step, 0)

        @pl.when(has_before)
        def _():
            for a in (0, 1):
                behind(a, c).start()

        for d in peers:
            outgoing(0, c, d).start()
        outgoing_local(0, c).start()

    def finish(c):
        cols = columns(c)

        @pl.when(has_after)
        def _():
            for a in (0, 1):
                behind(a, c).wait_recv()

        for a, own, back in ((1, own_key, back_key), (2, own_value, back_value)):
            results[a][:, cols] = (own[:, cols] + back[:, cols].astype(F32)).astype(BF16)
            for d in peers:
                outgoing(a, c, d).start()
            outgoing_local(a, c).start()

    forward(0)

    def chunk_step(c, carry):
        @pl.when(c + 1 < chunks)
        def _():
            forward(c + 1)

        @pl.when(c < chunks)
        def _():
            compute(c)

        @pl.when(c > 0)
        def _():
            finish(c - 1)

        return carry

    lax.fori_loop(0, chunks + 1, chunk_step, 0)

    def arrive(a):
        def wait(c, carry):
            for d in peers:
                outgoing(a, c, d).wait_recv()
            outgoing_local(a, c).wait()
            return carry

        lax.fori_loop(0, chunks, wait, 0)

    def norm_backward(raw_ref, row, inverse_ref, rows_ref, out_ref):
        gain_rows[...] = jnp.zeros_like(gain_rows)

        def block(i, carry):
            rows = pl.ds(pl.multiple_of(i * ROWS, ROWS), ROWS)
            inverse = inverse_ref[rows, :]
            normal = raw_ref[0, rows, :].astype(F32) * inverse
            upstream = rows_ref[rows, :].astype(F32)
            scaled = upstream * gain_full[row : row + 1, :]
            inner = jnp.sum(scaled * normal, axis=1, keepdims=True) * (1.0 / channels)
            out_ref[0, rows, :] = (inverse * (scaled - normal * inner)).astype(BF16)
            gain_rows[...] += upstream * normal
            return carry

        lax.fori_loop(0, tokens // ROWS, block, 0)
        gain_part[row : row + 1, :] = jnp.sum(gain_rows[...], axis=0, keepdims=True)

    arrive(0)
    norm_backward(query_ref, 0, q_inverse, dq_rows, query_out)
    arrive(1)
    norm_backward(key_ref, 1, k_inverse, dk_rows, key_out)

    def pair_copy(d):
        peer = lax.rem(f + d, n_fsdp)
        return remote(
            gain_part.at[:, pl.ds(pl.multiple_of(peer * part, HDIM), part)],
            pair_recv.at[d - 1], pair_s.at[d - 1], pair_r.at[d - 1], {"fsdp": peer},
        )

    for d in range(1, n_fsdp):
        pair_copy(d).start()
    arrive(2)
    value_out[0] = dv_rows[...]
    total = gain_part[:, pl.ds(pl.multiple_of(f * part, HDIM), part)]
    for d in range(1, n_fsdp):
        pair_copy(d).wait_recv()
        total = total + pair_recv[d - 1]
    tree_copies = []
    for b, (axis, device) in enumerate(tree):
        tree_send[b] = total
        copy = remote(
            tree_send.at[b], tree_recv.at[b], tree_s.at[b], tree_r.at[b], {axis: device}
        )
        copy.start()
        copy.wait_recv()
        total = tree_send[b] + tree_recv[b]
        tree_copies.append(copy)
    gain_out[...] = total

    for copy in tree_copies:
        copy.wait_send()
    for d in range(1, n_fsdp):
        gain_copy(d).wait_send()
        pair_copy(d).wait_send()

    def drain(c, carry):
        for d in peers:
            for a in range(4):
                incoming(a, c, d).wait_send()
            for a in range(3):
                outgoing(a, c, d).wait_send()

        @pl.when(has_after)
        def _():
            for a in (0, 1):
                ahead(a, c).wait_send()

        @pl.when(has_before)
        def _():
            for a in (0, 1):
                behind(a, c).wait_send()

        return carry

    lax.fori_loop(0, chunks, drain, 0)


def on_device(sizes, query_pre, key_pre, values, cotangent, gains, frame_span, denoise_steps):
    n_span, n_sp, n_fsdp = sizes
    _, tokens, channels = query_pre.shape
    group, width, part = tokens * n_sp, channels // n_sp, channels // n_fsdp
    heads = width // HDIM
    per_chunk = max(1, heads // 4)
    chunks = heads // per_chunk
    tree = max(1, (n_sp.bit_length() - 1) + (n_span.bit_length() - 1))
    vmem = pltpu.VMEM
    dma = pltpu.SemaphoreType.DMA
    scratch = [
        vmem((2, channels), F32),
        vmem((tokens, channels), BF16), vmem((tokens, channels), BF16),
        vmem((tokens, 1), F32), vmem((tokens, 1), F32),
        vmem((group, width), BF16), vmem((group, width), BF16),
        vmem((2 * group, width), BF16), vmem((2 * group, width), BF16),
        vmem((2 * group, group), F32), vmem((1, group), F32),
        vmem((group, width), F32), vmem((group, width), F32),
        vmem((group, width), BF16), vmem((group, width), BF16),
        vmem((group, width), BF16), vmem((group, width), BF16),
        vmem((group, width), BF16), vmem((group, width), BF16), vmem((group, width), BF16),
        vmem((tokens, channels), BF16), vmem((tokens, channels), BF16),
        vmem((tokens, channels), BF16),
        vmem((2, channels), F32), vmem((ROWS, channels), F32),
        vmem((max(1, n_fsdp - 1), 2, part), F32),
        vmem((tree, 2, part), F32), vmem((tree, 2, part), F32),
        dma((max(1, n_fsdp - 1),)), dma((max(1, n_fsdp - 1),)),
        dma((4, chunks, max(1, n_sp - 1))), dma((4, chunks, max(1, n_sp - 1))), dma((4,)),
        dma((2, chunks)), dma((2, chunks)), dma((2, chunks)), dma((2, chunks)),
        dma((3, chunks, max(1, n_sp - 1))), dma((3, chunks, max(1, n_sp - 1))),
        dma((3, chunks)),
        dma((max(1, n_fsdp - 1),)), dma((max(1, n_fsdp - 1),)), dma((tree,)), dma((tree,)),
    ]
    in_vmem = pl.BlockSpec(memory_space=pltpu.VMEM)
    pairs = heads * group * 2 * group
    return pl.pallas_call(
        functools.partial(kernel, (n_span, n_sp, n_fsdp, chunks, per_chunk)),
        out_shape=(
            jax.ShapeDtypeStruct(query_pre.shape, BF16),
            jax.ShapeDtypeStruct(query_pre.shape, BF16),
            jax.ShapeDtypeStruct(query_pre.shape, BF16),
            jax.ShapeDtypeStruct((2, part), F32),
        ),
        in_specs=[in_vmem] * 6 + [pl.BlockSpec(memory_space=pltpu.SMEM)],
        out_specs=[in_vmem] * 4,
        scratch_shapes=scratch,
        cost_estimate=pl.CostEstimate(
            flops=10 * pairs * HDIM, bytes_accessed=14 * tokens * channels, transcendentals=pairs
        ),
        compiler_params=pltpu.CompilerParams(
            collective_id=0, has_side_effects=True, vmem_limit_bytes=56 * 2**20
        ),
    )(query_pre, key_pre, values, cotangent, gains, frame_span, denoise_steps)


def solution(mesh):
    sizes = (mesh.shape["span"], mesh.shape["sp"], mesh.shape["fsdp"])
    rows = P("fsdp", ("span", "sp"), None)
    return jax.shard_map(
        functools.partial(on_device, sizes),
        mesh=mesh,
        in_specs=(rows, rows, rows, rows, P(None, "fsdp"), P("fsdp", "span"), P("fsdp", None)),
        out_specs=(rows, rows, rows, P(None, "fsdp")),
        check_vma=False,
    )
```

```python
import functools
import math

import jax
import jax.numpy as jnp
from jax import lax
from jax.experimental import pallas as pl
from jax.experimental.pallas import tpu as pltpu
from jax.sharding import PartitionSpec as P

HDIM = 128
EPSILON = 1e-06
NEGATIVE = -1e30
F32 = jnp.float32
BF16 = jnp.bfloat16
ROWS = 16


def dot(left, right, left_dim, right_dim):
    return lax.dot_general(
        left, right, (((left_dim,), (right_dim,)), ((), ())), preferred_element_type=F32
    )


def stages_of(devices):
    stages, stride = [], 1
    while devices > 1:
        size = next((n for n in (4, 2, 3) if devices % n == 0), devices)
        stages.append((stride, size))
        stride, devices = stride * size, devices // size
    return stages


def kernel(
    sizes,
    query_ref, key_ref, value_ref, grad_ref, gain_ref, span_ref, steps_ref,
    query_out, key_out, value_out, gain_out,
    gain_full, q_ready, k_ready, q_inverse, k_inverse,
    heads_query, heads_grad, key_joined, value_joined, bias, weight_row,
    own_key, own_value, send_key, send_value, back_key, back_value,
    dq_heads, dk_heads, dv_heads, dq_rows, dk_rows, dv_rows,
    gain_part, gain_rows, pair_recv, tree_send, tree_recv,
    gain_s, gain_r, in_s, in_r, in_local, ahead_s, ahead_r, behind_s, behind_r,
    out_s, out_r, out_local, pair_s, pair_r, tree_s, tree_r,
):
    n_span, n_sp, n_fsdp, chunks, per_chunk = sizes
    tokens, channels = q_ready.shape
    group, width = heads_query.shape
    part = channels // n_fsdp
    chunk_width = per_chunk * HDIM
    query_block = math.gcd(group, 256)
    scale = HDIM ** (-0.5)
    g, s, f = lax.axis_index("span"), lax.axis_index("sp"), lax.axis_index("fsdp")
    after, before = lax.rem(g + 1, n_span), lax.rem(g + n_span - 1, n_span)
    has_before, has_after = g > 0, g < n_span - 1

    place = g * n_sp + s

    def digit(stage):
        return lax.rem(lax.div(place, stage[0]), stage[1])

    def tree_peer(stage, d):
        mine = digit(stage)
        other = place + (lax.rem(mine + d, stage[1]) - mine) * stage[0]
        return {"span": lax.div(other, n_sp), "sp": lax.rem(other, n_sp)}

    tree = stages_of(n_span * n_sp)

    barrier = pltpu.get_barrier_semaphore()

    def greet(device):
        pl.semaphore_signal(
            barrier, inc=1, device_id=device, device_id_type=pl.DeviceIdType.MESH
        )

    count = 0
    for d in range(1, n_fsdp):
        greet({"fsdp": lax.rem(f + d, n_fsdp)})
        count += 1
    for d in range(1, n_sp):
        greet({"sp": lax.rem(s + d, n_sp)})
        count += 1
    for stage in tree:
        for d in range(1, stage[1]):
            greet(tree_peer(stage, d))
            count += 1

    @pl.when(has_before)
    def _():
        greet({"span": before})

    @pl.when(has_after)
    def _():
        greet({"span": after})

    count += lax.div(g + n_span - 1, n_span) + lax.div(2 * n_span - 2 - g, n_span)
    pl.semaphore_wait(barrier, count)

    def remote(src, dst, send, recv, device):
        return pltpu.make_async_remote_copy(
            src_ref=src, dst_ref=dst, send_sem=send, recv_sem=recv,
            device_id=device, device_id_type=pl.DeviceIdType.MESH,
        )

    def columns(c):
        return pl.ds(pl.multiple_of(c * chunk_width, HDIM), chunk_width)

    def shifted(base, c):
        return pl.ds(pl.multiple_of(base * width + c * chunk_width, HDIM), chunk_width)

    def row_block(index):
        return pl.ds(pl.multiple_of(index * tokens, tokens), tokens)

    sources = (k_ready, value_ref.at[0], q_ready, grad_ref.at[0])
    homes = (key_joined, value_joined, heads_query, heads_grad)

    def incoming(a, c, d):
        peer = lax.rem(s + d, n_sp)
        return remote(
            sources[a].at[:, shifted(peer, c)], homes[a].at[row_block(s), columns(c)],
            in_s.at[a, c, d - 1], in_r.at[a, c, d - 1], {"sp": peer},
        )

    def incoming_local(a):
        return pltpu.make_async_copy(
            sources[a].at[:, pl.ds(pl.multiple_of(s * width, HDIM), width)],
            homes[a].at[row_block(s), :], in_local.at[a],
        )

    def ahead(a, c):
        home = homes[a]
        return remote(
            home.at[pl.ds(0, group), columns(c)], home.at[pl.ds(group, group), columns(c)],
            ahead_s.at[a, c], ahead_r.at[a, c], {"span": after},
        )

    def behind(a, c):
        return remote(
            (send_key, send_value)[a].at[:, columns(c)],
            (back_key, back_value)[a].at[:, columns(c)],
            behind_s.at[a, c], behind_r.at[a, c], {"span": before},
        )

    results = (dq_heads, dk_heads, dv_heads)
    landed = (dq_rows, dk_rows, dv_rows)

    def outgoing(a, c, d):
        peer = lax.rem(s + d, n_sp)
        return remote(
            results[a].at[row_block(peer), columns(c)], landed[a].at[:, shifted(s, c)],
            out_s.at[a, c, d - 1], out_r.at[a, c, d - 1], {"sp": peer},
        )

    def outgoing_local(a, c):
        return pltpu.make_async_copy(
            results[a].at[row_block(s), columns(c)], landed[a].at[:, shifted(s, c)],
            out_local.at[a, c],
        )

    def gain_copy(d):
        mine = pl.ds(pl.multiple_of(f * part, HDIM), part)
        return remote(
            gain_ref, gain_full.at[:, mine], gain_s.at[d - 1], gain_r.at[d - 1],
            {"fsdp": lax.rem(f + d, n_fsdp)},
        )

    peers = range(1, n_sp)
    for d in range(1, n_fsdp):
        gain_copy(d).start()
    early = min(3, chunks)

    def start_early(a):
        for c in range(early):
            for d in peers:
                incoming(a, c, d).start()
        incoming_local(a).start()

    start_early(1)
    start_early(3)
    gain_full[:, pl.ds(pl.multiple_of(f * part, HDIM), part)] = gain_ref[...]

    @pl.when(g == 0)
    def _():
        key_joined[group:, :] = jnp.zeros((group, width), BF16)
        value_joined[group:, :] = jnp.zeros((group, width), BF16)

    @pl.when(g == n_span - 1)
    def _():
        back_key[...] = jnp.zeros_like(back_key)
        back_value[...] = jnp.zeros_like(back_value)

    for d in range(1, n_fsdp):
        gain_copy(d).wait_recv()

    def norm(raw_ref, row, inverse_ref, ready_ref):
        def block(i, carry):
            rows = pl.ds(pl.multiple_of(i * ROWS, ROWS), ROWS)
            wide = raw_ref[0, rows, :].astype(F32)
            inverse = lax.rsqrt(
                jnp.sum(wide * wide, axis=1, keepdims=True) * (1.0 / channels) + EPSILON
            )
            inverse_ref[rows, :] = inverse
            ready_ref[rows, :] = (wide * inverse * gain_full[row : row + 1, :]).astype(BF16)
            return carry

        lax.fori_loop(0, tokens // ROWS, block, 0)

    norm(key_ref, 1, k_inverse, k_ready)
    start_early(0)
    norm(query_ref, 0, q_inverse, q_ready)
    start_early(2)

    def start_chunk(c, carry):
        for a in range(4):
            for d in peers:
                incoming(a, c, d).start()
        return carry

    lax.fori_loop(early, chunks, start_chunk, 0)

    ids = span_ref[...]
    ids_down = jnp.transpose(jnp.broadcast_to(ids.astype(F32), (HDIM, group)))[:, :1]
    bias[:group, :] = jnp.where(ids_down <= ids.astype(F32), 0.0, NEGATIVE)
    bias[group:, :] = jnp.zeros((group, group), F32) + jnp.where(has_before, 0.0, NEGATIVE)
    weight = jnp.zeros(ids.shape, F32)
    for index in range(steps_ref.shape[1]):
        weight = jnp.where(ids == index, steps_ref[0, index].astype(F32), weight)
    weight_row[...] = weight

    for a in range(4):
        incoming_local(a).wait()

    def forward(c):
        for a in (0, 1):
            for d in peers:
                incoming(a, c, d).wait_recv()

            @pl.when(has_after)
            def _():
                ahead(a, c).start()

    def one_block(head, block_index):
        cols = pl.ds(pl.multiple_of(head * HDIM, HDIM), HDIM)
        if query_block == group:
            rows = pl.ds(0, group)
        else:
            rows = pl.ds(pl.multiple_of(block_index * query_block, query_block), query_block)
        query = heads_query[rows, cols]
        grad = heads_grad[rows, cols]
        keys = key_joined[:, cols]
        scores = dot(keys, query, 1, 1) * (scale * math.log2(math.e)) + bias[:, rows]
        top = jnp.max(scores, axis=0, keepdims=True)
        raised = jnp.exp2(scores - top)
        inverse_total = 1.0 / jnp.sum(raised, axis=0, keepdims=True)
        grad_prob = dot(value_joined[:, cols], grad, 1, 1)
        delta = jnp.sum(raised * grad_prob, axis=0, keepdims=True) * inverse_total
        weighted = raised * (weight_row[:, rows] * inverse_total)
        sgrad = (weighted * (grad_prob - delta)).astype(BF16)
        weights = weighted.astype(BF16)
        dq_heads[rows, cols] = (dot(sgrad, keys, 0, 0) * scale).astype(BF16)
        return dot(sgrad, query, 1, 0) * scale, dot(weights, grad, 1, 0)

    def one_head(head):
        cols = pl.ds(pl.multiple_of(head * HDIM, HDIM), HDIM)
        if query_block == group:
            key_term, value_term = one_block(head, 0)
        else:
            zero = jnp.zeros((2 * group, HDIM), F32)

            def add(i, total):
                terms = one_block(head, i)
                return total[0] + terms[0], total[1] + terms[1]

            key_term, value_term = lax.fori_loop(0, group // query_block, add, (zero, zero))
        own_key[:, cols] = key_term[:group]
        own_value[:, cols] = value_term[:group]
        send_key[:, cols] = key_term[group:].astype(BF16)
        send_value[:, cols] = value_term[group:].astype(BF16)

    def compute(c):
        for a in (2, 3):
            for d in peers:
                incoming(a, c, d).wait_recv()

        @pl.when(has_before)
        def _():
            for a in (0, 1):
                ahead(a, c).wait_recv()

        def head_step(i, carry):
            one_head(c * per_chunk + i)
            return carry

        lax.fori_loop(0, per_chunk, head_step, 0)

        @pl.when(has_before)
        def _():
            for a in (0, 1):
                behind(a, c).start()

        for d in peers:
            outgoing(0, c, d).start()
        outgoing_local(0, c).start()

    def finish(c):
        cols = columns(c)

        @pl.when(has_after)
        def _():
            for a in (0, 1):
                behind(a, c).wait_recv()

        for a, own, back in ((1, own_key, back_key), (2, own_value, back_value)):
            results[a][:, cols] = (own[:, cols] + back[:, cols].astype(F32)).astype(BF16)
            for d in peers:
                outgoing(a, c, d).start()
            outgoing_local(a, c).start()

    lead = min(2, chunks)
    for c in range(lead):
        forward(c)

    def chunk_step(c, carry):
        @pl.when(c + lead < chunks)
        def _():
            forward(c + lead)

        @pl.when(c < chunks)
        def _():
            compute(c)

        @pl.when(c >= lead)
        def _():
            finish(c - lead)

        return carry

    lax.fori_loop(0, chunks + lead, chunk_step, 0)

    def arrive(a):
        def wait(c, carry):
            for d in peers:
                outgoing(a, c, d).wait_recv()
            outgoing_local(a, c).wait()
            return carry

        lax.fori_loop(0, chunks, wait, 0)

    def norm_backward(raw_ref, row, inverse_ref, rows_ref, out_ref):
        gain_rows[...] = jnp.zeros_like(gain_rows)

        def block(i, carry):
            rows = pl.ds(pl.multiple_of(i * ROWS, ROWS), ROWS)
            inverse = inverse_ref[rows, :]
            normal = raw_ref[0, rows, :].astype(F32) * inverse
            upstream = rows_ref[rows, :].astype(F32)
            scaled = upstream * gain_full[row : row + 1, :]
            inner = jnp.sum(scaled * normal, axis=1, keepdims=True) * (1.0 / channels)
            out_ref[0, rows, :] = (inverse * (scaled - normal * inner)).astype(BF16)
            gain_rows[...] += upstream * normal
            return carry

        lax.fori_loop(0, tokens // ROWS, block, 0)
        gain_part[row : row + 1, :] = jnp.sum(gain_rows[...], axis=0, keepdims=True)

    arrive(0)
    norm_backward(query_ref, 0, q_inverse, dq_rows, query_out)
    arrive(1)
    norm_backward(key_ref, 1, k_inverse, dk_rows, key_out)

    def pair_copy(d):
        peer = lax.rem(f + d, n_fsdp)
        return remote(
            gain_part.at[:, pl.ds(pl.multiple_of(peer * part, HDIM), part)],
            pair_recv.at[d - 1], pair_s.at[d - 1], pair_r.at[d - 1], {"fsdp": peer},
        )

    for d in range(1, n_fsdp):
        pair_copy(d).start()
    arrive(2)
    value_out[0] = dv_rows[...]
    total = gain_part[:, pl.ds(pl.multiple_of(f * part, HDIM), part)]
    for d in range(1, n_fsdp):
        pair_copy(d).wait_recv()
        total = total + pair_recv[d - 1]
    tree_copies = []
    for b, stage in enumerate(tree):
        tree_send[b] = total
        copies = [
            remote(
                tree_send.at[b], tree_recv.at[b, digit(stage)],
                tree_s.at[b, d - 1], tree_r.at[b, d - 1], tree_peer(stage, d),
            )
            for d in range(1, stage[1])
        ]
        for copy in copies:
            copy.start()
        tree_recv[b, digit(stage)] = total
        for copy in copies:
            copy.wait_recv()
        total = tree_recv[b, 0]
        for index in range(1, stage[1]):
            total = total + tree_recv[b, index]
        tree_copies += copies
    gain_out[...] = total

    for copy in tree_copies:
        copy.wait_send()
    for d in range(1, n_fsdp):
        gain_copy(d).wait_send()
        pair_copy(d).wait_send()

    def drain(c, carry):
        for d in peers:
            for a in range(4):
                incoming(a, c, d).wait_send()
            for a in range(3):
                outgoing(a, c, d).wait_send()

        @pl.when(has_after)
        def _():
            for a in (0, 1):
                ahead(a, c).wait_send()

        @pl.when(has_before)
        def _():
            for a in (0, 1):
                behind(a, c).wait_send()

        return carry

    lax.fori_loop(0, chunks, drain, 0)


def on_device(sizes, query_pre, key_pre, values, cotangent, gains, frame_span, denoise_steps):
    n_span, n_sp, n_fsdp = sizes
    _, tokens, channels = query_pre.shape
    group, width, part = tokens * n_sp, channels // n_sp, channels // n_fsdp
    heads = width // HDIM
    per_chunk = 1
    chunks = heads // per_chunk
    stages = stages_of(n_span * n_sp)
    tree = max(1, len(stages))
    most = max([size for _, size in stages] + [2])
    vmem = pltpu.VMEM
    dma = pltpu.SemaphoreType.DMA
    scratch = [
        vmem((2, channels), F32),
        vmem((tokens, channels), BF16), vmem((tokens, channels), BF16),
        vmem((tokens, 1), F32), vmem((tokens, 1), F32),
        vmem((group, width), BF16), vmem((group, width), BF16),
        vmem((2 * group, width), BF16), vmem((2 * group, width), BF16),
        vmem((2 * group, group), F32), vmem((1, group), F32),
        vmem((group, width), F32), vmem((group, width), F32),
        vmem((group, width), BF16), vmem((group, width), BF16),
        vmem((group, width), BF16), vmem((group, width), BF16),
        vmem((group, width), BF16), vmem((group, width), BF16), vmem((group, width), BF16),
        vmem((tokens, channels), BF16), vmem((tokens, channels), BF16),
        vmem((tokens, channels), BF16),
        vmem((2, channels), F32), vmem((ROWS, channels), F32),
        vmem((max(1, n_fsdp - 1), 2, part), F32),
        vmem((tree, 2, part), F32), vmem((tree, most, 2, part), F32),
        dma((max(1, n_fsdp - 1),)), dma((max(1, n_fsdp - 1),)),
        dma((4, chunks, max(1, n_sp - 1))), dma((4, chunks, max(1, n_sp - 1))), dma((4,)),
        dma((2, chunks)), dma((2, chunks)), dma((2, chunks)), dma((2, chunks)),
        dma((3, chunks, max(1, n_sp - 1))), dma((3, chunks, max(1, n_sp - 1))),
        dma((3, chunks)),
        dma((max(1, n_fsdp - 1),)), dma((max(1, n_fsdp - 1),)), dma((tree, most - 1)),
        dma((tree, most - 1)),
    ]
    in_vmem = pl.BlockSpec(memory_space=pltpu.VMEM)
    pairs = heads * group * 2 * group
    return pl.pallas_call(
        functools.partial(kernel, (n_span, n_sp, n_fsdp, chunks, per_chunk)),
        out_shape=(
            jax.ShapeDtypeStruct(query_pre.shape, BF16),
            jax.ShapeDtypeStruct(query_pre.shape, BF16),
            jax.ShapeDtypeStruct(query_pre.shape, BF16),
            jax.ShapeDtypeStruct((2, part), F32),
        ),
        in_specs=[in_vmem] * 6 + [pl.BlockSpec(memory_space=pltpu.SMEM)],
        out_specs=[in_vmem] * 4,
        scratch_shapes=scratch,
        cost_estimate=pl.CostEstimate(
            flops=10 * pairs * HDIM, bytes_accessed=14 * tokens * channels, transcendentals=pairs
        ),
        compiler_params=pltpu.CompilerParams(
            collective_id=0, has_side_effects=True, vmem_limit_bytes=56 * 2**20
        ),
    )(query_pre, key_pre, values, cotangent, gains, frame_span, denoise_steps)


def solution(mesh):
    sizes = (mesh.shape["span"], mesh.shape["sp"], mesh.shape["fsdp"])
    rows = P("fsdp", ("span", "sp"), None)
    return jax.shard_map(
        functools.partial(on_device, sizes),
        mesh=mesh,
        in_specs=(rows, rows, rows, rows, P(None, "fsdp"), P("fsdp", "span"), P("fsdp", None)),
        out_specs=(rows, rows, rows, P(None, "fsdp")),
        check_vma=False,
    )
```

```python
import functools
import math

import jax
import jax.numpy as jnp
from jax import lax
from jax.experimental import pallas as pl
from jax.experimental.pallas import tpu as pltpu
from jax.sharding import PartitionSpec as P

HDIM = 128
EPSILON = 1e-06
NEGATIVE = -1e30
F32 = jnp.float32
BF16 = jnp.bfloat16
ROWS = 16


def dot(left, right, left_dim, right_dim):
    return lax.dot_general(
        left, right, (((left_dim,), (right_dim,)), ((), ())), preferred_element_type=F32
    )


def stages_of(devices):
    stages, stride = [], 1
    while devices > 1:
        size = next((n for n in (4, 2, 3) if devices % n == 0), devices)
        stages.append((stride, size))
        stride, devices = stride * size, devices // size
    return stages


def kernel(
    sizes,
    query_ref, key_ref, value_ref, grad_ref, gain_ref, span_ref, steps_ref,
    query_out, key_out, value_out, gain_out,
    gain_full, q_ready, k_ready, q_inverse, k_inverse,
    heads_query, heads_grad, key_joined, value_joined, bias, weight_row,
    own_key, own_value, send_key, send_value, back_key, back_value,
    dq_heads, dk_heads, dv_heads, dq_rows, dk_rows, dv_rows,
    gain_part, gain_rows, pair_recv, tree_send, tree_recv,
    gain_s, gain_r, in_s, in_r, in_local, ahead_s, ahead_r, behind_s, behind_r,
    out_s, out_r, out_local, pair_s, pair_r, tree_s, tree_r,
):
    n_span, n_sp, n_fsdp, chunks, per_chunk = sizes
    tokens, channels = q_ready.shape
    group, width = heads_query.shape
    part = channels // n_fsdp
    chunk_width = per_chunk * HDIM
    query_block = math.gcd(group, 256)
    scale = HDIM ** (-0.5)
    g, s, f = lax.axis_index("span"), lax.axis_index("sp"), lax.axis_index("fsdp")
    after, before = lax.rem(g + 1, n_span), lax.rem(g + n_span - 1, n_span)
    has_before, has_after = g > 0, g < n_span - 1

    place = g * n_sp + s

    def digit(stage):
        return lax.rem(lax.div(place, stage[0]), stage[1])

    def tree_peer(stage, d):
        mine = digit(stage)
        other = place + (lax.rem(mine + d, stage[1]) - mine) * stage[0]
        return {"span": lax.div(other, n_sp), "sp": lax.rem(other, n_sp)}

    tree = stages_of(n_span * n_sp)

    barrier = pltpu.get_barrier_semaphore()

    def greet(device):
        pl.semaphore_signal(
            barrier, inc=1, device_id=device, device_id_type=pl.DeviceIdType.MESH
        )

    count = 0
    for d in range(1, n_fsdp):
        greet({"fsdp": lax.rem(f + d, n_fsdp)})
        count += 1
    for d in range(1, n_sp):
        greet({"sp": lax.rem(s + d, n_sp)})
        count += 1
    for stage in tree:
        for d in range(1, stage[1]):
            greet(tree_peer(stage, d))
            count += 1

    @pl.when(has_before)
    def _():
        greet({"span": before})

    @pl.when(has_after)
    def _():
        greet({"span": after})

    count += lax.div(g + n_span - 1, n_span) + lax.div(2 * n_span - 2 - g, n_span)
    pl.semaphore_wait(barrier, count)

    def remote(src, dst, send, recv, device):
        return pltpu.make_async_remote_copy(
            src_ref=src, dst_ref=dst, send_sem=send, recv_sem=recv,
            device_id=device, device_id_type=pl.DeviceIdType.MESH,
        )

    def columns(c):
        return pl.ds(pl.multiple_of(c * chunk_width, HDIM), chunk_width)

    def shifted(base, c):
        return pl.ds(pl.multiple_of(base * width + c * chunk_width, HDIM), chunk_width)

    def row_block(index):
        return pl.ds(pl.multiple_of(index * tokens, tokens), tokens)

    sources = (k_ready, value_ref.at[0], q_ready, grad_ref.at[0])
    homes = (key_joined, value_joined, heads_query, heads_grad)

    def incoming(a, c, d):
        peer = lax.rem(s + d, n_sp)
        return remote(
            sources[a].at[:, shifted(peer, c)], homes[a].at[row_block(s), columns(c)],
            in_s.at[a, c, d - 1], in_r.at[a, c, d - 1], {"sp": peer},
        )

    def incoming_local(a):
        return pltpu.make_async_copy(
            sources[a].at[:, pl.ds(pl.multiple_of(s * width, HDIM), width)],
            homes[a].at[row_block(s), :], in_local.at[a],
        )

    def ahead(a, c):
        home = homes[a]
        return remote(
            home.at[pl.ds(0, group), columns(c)], home.at[pl.ds(group, group), columns(c)],
            ahead_s.at[a, c], ahead_r.at[a, c], {"span": after},
        )

    def behind(a, c):
        return remote(
            (send_key, send_value)[a].at[:, columns(c)],
            (back_key, back_value)[a].at[:, columns(c)],
            behind_s.at[a, c], behind_r.at[a, c], {"span": before},
        )

    results = (dq_heads, dk_heads, dv_heads)
    landed = (dq_rows, dk_rows, dv_rows)

    def outgoing(a, c, d):
        peer = lax.rem(s + d, n_sp)
        return remote(
            results[a].at[row_block(peer), columns(c)], landed[a].at[:, shifted(s, c)],
            out_s.at[a, c, d - 1], out_r.at[a, c, d - 1], {"sp": peer},
        )

    def outgoing_local(a, c):
        return pltpu.make_async_copy(
            results[a].at[row_block(s), columns(c)], landed[a].at[:, shifted(s, c)],
            out_local.at[a, c],
        )

    def gain_copy(d):
        mine = pl.ds(pl.multiple_of(f * part, HDIM), part)
        return remote(
            gain_ref, gain_full.at[:, mine], gain_s.at[d - 1], gain_r.at[d - 1],
            {"fsdp": lax.rem(f + d, n_fsdp)},
        )

    peers = range(1, n_sp)
    for d in range(1, n_fsdp):
        gain_copy(d).start()
    early = min(3, chunks)

    def start_early(a):
        for c in range(early):
            for d in peers:
                incoming(a, c, d).start()
        incoming_local(a).start()

    start_early(1)
    start_early(3)
    gain_full[:, pl.ds(pl.multiple_of(f * part, HDIM), part)] = gain_ref[...]

    @pl.when(g == 0)
    def _():
        key_joined[group:, :] = jnp.zeros((group, width), BF16)
        value_joined[group:, :] = jnp.zeros((group, width), BF16)

    @pl.when(g == n_span - 1)
    def _():
        back_key[...] = jnp.zeros_like(back_key)
        back_value[...] = jnp.zeros_like(back_value)

    for d in range(1, n_fsdp):
        gain_copy(d).wait_recv()

    def norm(raw_ref, row, inverse_ref, ready_ref):
        def block(i, carry):
            rows = pl.ds(pl.multiple_of(i * ROWS, ROWS), ROWS)
            wide = raw_ref[0, rows, :].astype(F32)
            inverse = lax.rsqrt(
                jnp.sum(wide * wide, axis=1, keepdims=True) * (1.0 / channels) + EPSILON
            )
            inverse_ref[rows, :] = inverse
            ready_ref[rows, :] = (wide * inverse * gain_full[row : row + 1, :]).astype(BF16)
            return carry

        lax.fori_loop(0, tokens // ROWS, block, 0)

    norm(key_ref, 1, k_inverse, k_ready)
    start_early(0)
    norm(query_ref, 0, q_inverse, q_ready)
    start_early(2)

    def start_chunk(c, carry):
        for a in range(4):
            for d in peers:
                incoming(a, c, d).start()
        return carry

    lax.fori_loop(early, chunks, start_chunk, 0)

    ids = span_ref[...]
    ids_down = jnp.transpose(jnp.broadcast_to(ids.astype(F32), (HDIM, group)))[:, :1]
    bias[:group, :] = jnp.where(ids_down <= ids.astype(F32), 0.0, NEGATIVE)
    bias[group:, :] = jnp.zeros((group, group), F32) + jnp.where(has_before, 0.0, NEGATIVE)
    weight = jnp.zeros(ids.shape, F32)
    for index in range(steps_ref.shape[1]):
        weight = jnp.where(ids == index, steps_ref[0, index].astype(F32), weight)
    weight_row[...] = weight

    for a in range(4):
        incoming_local(a).wait()

    def forward(c):
        for a in (0, 1):
            for d in peers:
                incoming(a, c, d).wait_recv()

            @pl.when(has_after)
            def _():
                ahead(a, c).start()

    def one_block(head, block_index):
        cols = pl.ds(pl.multiple_of(head * HDIM, HDIM), HDIM)
        if query_block == group:
            rows = pl.ds(0, group)
        else:
            rows = pl.ds(pl.multiple_of(block_index * query_block, query_block), query_block)
        query = heads_query[rows, cols]
        grad = heads_grad[rows, cols]
        keys = key_joined[:, cols]
        scores = dot(keys, query, 1, 1) * (scale * math.log2(math.e)) + bias[:, rows]
        top = jnp.max(scores, axis=0, keepdims=True)
        raised = jnp.exp2(scores - top)
        inverse_total = 1.0 / jnp.sum(raised, axis=0, keepdims=True)
        grad_prob = dot(value_joined[:, cols], grad, 1, 1)
        delta = jnp.sum(raised * grad_prob, axis=0, keepdims=True) * inverse_total
        weighted = raised * (weight_row[:, rows] * inverse_total)
        sgrad = (weighted * (grad_prob - delta)).astype(BF16)
        weights = weighted.astype(BF16)
        dq_heads[rows, cols] = (dot(sgrad, keys, 0, 0) * scale).astype(BF16)
        return dot(sgrad, query, 1, 0) * scale, dot(weights, grad, 1, 0)

    def one_head(head):
        cols = pl.ds(pl.multiple_of(head * HDIM, HDIM), HDIM)
        if query_block == group:
            key_term, value_term = one_block(head, 0)
        else:
            zero = jnp.zeros((2 * group, HDIM), F32)

            def add(i, total):
                terms = one_block(head, i)
                return total[0] + terms[0], total[1] + terms[1]

            key_term, value_term = lax.fori_loop(0, group // query_block, add, (zero, zero))
        own_key[:, cols] = key_term[:group]
        own_value[:, cols] = value_term[:group]
        send_key[:, cols] = key_term[group:].astype(BF16)
        send_value[:, cols] = value_term[group:].astype(BF16)

    def compute(c):
        for a in (2, 3):
            for d in peers:
                incoming(a, c, d).wait_recv()

        @pl.when(has_before)
        def _():
            for a in (0, 1):
                ahead(a, c).wait_recv()

        def head_step(i, carry):
            one_head(c * per_chunk + i)
            return carry

        lax.fori_loop(0, per_chunk, head_step, 0)

        @pl.when(has_before)
        def _():
            for a in (0, 1):
                behind(a, c).start()

        for d in peers:
            outgoing(0, c, d).start()
        outgoing_local(0, c).start()

    def finish(c):
        cols = columns(c)

        @pl.when(has_after)
        def _():
            for a in (0, 1):
                behind(a, c).wait_recv()

        for a, own, back in ((1, own_key, back_key), (2, own_value, back_value)):
            results[a][:, cols] = (own[:, cols] + back[:, cols].astype(F32)).astype(BF16)
            for d in peers:
                outgoing(a, c, d).start()
            outgoing_local(a, c).start()

    lead = min(3, chunks)
    lag = min(3, chunks)
    for c in range(lead):
        forward(c)

    def chunk_step(c, carry):
        @pl.when(c + lead < chunks)
        def _():
            forward(c + lead)

        @pl.when(c < chunks)
        def _():
            compute(c)

        @pl.when(c >= lag)
        def _():
            finish(c - lag)

        return carry

    lax.fori_loop(0, chunks + lag, chunk_step, 0)

    def arrive(a):
        def wait(c, carry):
            for d in peers:
                outgoing(a, c, d).wait_recv()
            outgoing_local(a, c).wait()
            return carry

        lax.fori_loop(0, chunks, wait, 0)

    def norm_backward(raw_ref, row, inverse_ref, rows_ref, out_ref):
        gain_rows[...] = jnp.zeros_like(gain_rows)

        def block(i, carry):
            rows = pl.ds(pl.multiple_of(i * ROWS, ROWS), ROWS)
            inverse = inverse_ref[rows, :]
            normal = raw_ref[0, rows, :].astype(F32) * inverse
            upstream = rows_ref[rows, :].astype(F32)
            scaled = upstream * gain_full[row : row + 1, :]
            inner = jnp.sum(scaled * normal, axis=1, keepdims=True) * (1.0 / channels)
            out_ref[0, rows, :] = (inverse * (scaled - normal * inner)).astype(BF16)
            gain_rows[...] += upstream * normal
            return carry

        lax.fori_loop(0, tokens // ROWS, block, 0)
        gain_part[row : row + 1, :] = jnp.sum(gain_rows[...], axis=0, keepdims=True)

    arrive(0)
    norm_backward(query_ref, 0, q_inverse, dq_rows, query_out)
    arrive(1)
    norm_backward(key_ref, 1, k_inverse, dk_rows, key_out)

    def pair_copy(d):
        peer = lax.rem(f + d, n_fsdp)
        return remote(
            gain_part.at[:, pl.ds(pl.multiple_of(peer * part, HDIM), part)],
            pair_recv.at[d - 1], pair_s.at[d - 1], pair_r.at[d - 1], {"fsdp": peer},
        )

    for d in range(1, n_fsdp):
        pair_copy(d).start()
    arrive(2)
    value_out[0] = dv_rows[...]
    total = gain_part[:, pl.ds(pl.multiple_of(f * part, HDIM), part)]
    for d in range(1, n_fsdp):
        pair_copy(d).wait_recv()
        total = total + pair_recv[d - 1]
    tree_copies = []
    for b, stage in enumerate(tree):
        tree_send[b] = total
        copies = [
            remote(
                tree_send.at[b], tree_recv.at[b, digit(stage)],
                tree_s.at[b, d - 1], tree_r.at[b, d - 1], tree_peer(stage, d),
            )
            for d in range(1, stage[1])
        ]
        for copy in copies:
            copy.start()
        tree_recv[b, digit(stage)] = total
        for copy in copies:
            copy.wait_recv()
        total = tree_recv[b, 0]
        for index in range(1, stage[1]):
            total = total + tree_recv[b, index]
        tree_copies += copies
    gain_out[...] = total

    for copy in tree_copies:
        copy.wait_send()
    for d in range(1, n_fsdp):
        gain_copy(d).wait_send()
        pair_copy(d).wait_send()

    def drain(c, carry):
        for d in peers:
            for a in range(4):
                incoming(a, c, d).wait_send()
            for a in range(3):
                outgoing(a, c, d).wait_send()

        @pl.when(has_after)
        def _():
            for a in (0, 1):
                ahead(a, c).wait_send()

        @pl.when(has_before)
        def _():
            for a in (0, 1):
                behind(a, c).wait_send()

        return carry

    lax.fori_loop(0, chunks, drain, 0)


def on_device(sizes, query_pre, key_pre, values, cotangent, gains, frame_span, denoise_steps):
    n_span, n_sp, n_fsdp = sizes
    _, tokens, channels = query_pre.shape
    group, width, part = tokens * n_sp, channels // n_sp, channels // n_fsdp
    heads = width // HDIM
    per_chunk = 1
    chunks = heads // per_chunk
    stages = stages_of(n_span * n_sp)
    tree = max(1, len(stages))
    most = max([size for _, size in stages] + [2])
    vmem = pltpu.VMEM
    dma = pltpu.SemaphoreType.DMA
    scratch = [
        vmem((2, channels), F32),
        vmem((tokens, channels), BF16), vmem((tokens, channels), BF16),
        vmem((tokens, 1), F32), vmem((tokens, 1), F32),
        vmem((group, width), BF16), vmem((group, width), BF16),
        vmem((2 * group, width), BF16), vmem((2 * group, width), BF16),
        vmem((2 * group, group), F32), vmem((1, group), F32),
        vmem((group, width), F32), vmem((group, width), F32),
        vmem((group, width), BF16), vmem((group, width), BF16),
        vmem((group, width), BF16), vmem((group, width), BF16),
        vmem((group, width), BF16), vmem((group, width), BF16), vmem((group, width), BF16),
        vmem((tokens, channels), BF16), vmem((tokens, channels), BF16),
        vmem((tokens, channels), BF16),
        vmem((2, channels), F32), vmem((ROWS, channels), F32),
        vmem((max(1, n_fsdp - 1), 2, part), F32),
        vmem((tree, 2, part), F32), vmem((tree, most, 2, part), F32),
        dma((max(1, n_fsdp - 1),)), dma((max(1, n_fsdp - 1),)),
        dma((4, chunks, max(1, n_sp - 1))), dma((4, chunks, max(1, n_sp - 1))), dma((4,)),
        dma((2, chunks)), dma((2, chunks)), dma((2, chunks)), dma((2, chunks)),
        dma((3, chunks, max(1, n_sp - 1))), dma((3, chunks, max(1, n_sp - 1))),
        dma((3, chunks)),
        dma((max(1, n_fsdp - 1),)), dma((max(1, n_fsdp - 1),)), dma((tree, most - 1)),
        dma((tree, most - 1)),
    ]
    in_vmem = pl.BlockSpec(memory_space=pltpu.VMEM)
    pairs = heads * group * 2 * group
    return pl.pallas_call(
        functools.partial(kernel, (n_span, n_sp, n_fsdp, chunks, per_chunk)),
        out_shape=(
            jax.ShapeDtypeStruct(query_pre.shape, BF16),
            jax.ShapeDtypeStruct(query_pre.shape, BF16),
            jax.ShapeDtypeStruct(query_pre.shape, BF16),
            jax.ShapeDtypeStruct((2, part), F32),
        ),
        in_specs=[in_vmem] * 6 + [pl.BlockSpec(memory_space=pltpu.SMEM)],
        out_specs=[in_vmem] * 4,
        scratch_shapes=scratch,
        cost_estimate=pl.CostEstimate(
            flops=10 * pairs * HDIM, bytes_accessed=14 * tokens * channels, transcendentals=pairs
        ),
        compiler_params=pltpu.CompilerParams(
            collective_id=0, has_side_effects=True, vmem_limit_bytes=56 * 2**20
        ),
    )(query_pre, key_pre, values, cotangent, gains, frame_span, denoise_steps)


def solution(mesh):
    sizes = (mesh.shape["span"], mesh.shape["sp"], mesh.shape["fsdp"])
    rows = P("fsdp", ("span", "sp"), None)
    return jax.shard_map(
        functools.partial(on_device, sizes),
        mesh=mesh,
        in_specs=(rows, rows, rows, rows, P(None, "fsdp"), P("fsdp", "span"), P("fsdp", None)),
        out_specs=(rows, rows, rows, P(None, "fsdp")),
        check_vma=False,
    )
```

```python
import functools
import math

import jax
import jax.numpy as jnp
from jax import lax
from jax.experimental import pallas as pl
from jax.experimental.pallas import tpu as pltpu
from jax.sharding import PartitionSpec as P

HDIM = 128
EPSILON = 1e-06
NEGATIVE = -1e30
F32 = jnp.float32
BF16 = jnp.bfloat16
ROWS = 16


def dot(left, right, left_dim, right_dim):
    return lax.dot_general(
        left, right, (((left_dim,), (right_dim,)), ((), ())), preferred_element_type=F32
    )


def stages_of(devices):
    stages, stride = [], 1
    while devices > 1:
        size = next((n for n in (4, 2, 3) if devices % n == 0), devices)
        stages.append((stride, size))
        stride, devices = stride * size, devices // size
    return stages


def kernel(
    sizes,
    query_ref, key_ref, value_ref, grad_ref, gain_ref, span_ref, steps_ref,
    query_out, key_out, value_out, gain_out,
    gain_full, q_ready, k_ready, q_inverse, k_inverse,
    heads_query, heads_grad, key_joined, value_joined, bias, weight_row,
    own_key, own_value, send_key, send_value, back_key, back_value,
    dq_heads, dk_heads, dv_heads, dq_rows, dk_rows, dv_rows,
    gain_part, gain_rows, pair_recv, tree_send, tree_recv,
    gain_s, gain_r, in_s, in_r, in_local, ahead_s, ahead_r, behind_s, behind_r,
    out_s, out_r, out_local, pair_s, pair_r, tree_s, tree_r,
):
    n_span, n_sp, n_fsdp, chunks, per_chunk = sizes
    tokens, channels = q_ready.shape
    group, width = heads_query.shape
    part = channels // n_fsdp
    chunk_width = per_chunk * HDIM
    query_block = math.gcd(group, 256)
    scale = HDIM ** (-0.5)
    g, s, f = lax.axis_index("span"), lax.axis_index("sp"), lax.axis_index("fsdp")
    after, before = lax.rem(g + 1, n_span), lax.rem(g + n_span - 1, n_span)
    has_before, has_after = g > 0, g < n_span - 1

    place = g * n_sp + s

    def digit(stage):
        return lax.rem(lax.div(place, stage[0]), stage[1])

    def tree_peer(stage, d):
        mine = digit(stage)
        other = place + (lax.rem(mine + d, stage[1]) - mine) * stage[0]
        return {"span": lax.div(other, n_sp), "sp": lax.rem(other, n_sp)}

    tree = stages_of(n_span * n_sp)

    barrier = pltpu.get_barrier_semaphore()

    def greet(device):
        pl.semaphore_signal(
            barrier, inc=1, device_id=device, device_id_type=pl.DeviceIdType.MESH
        )

    count = 0
    for d in range(1, n_fsdp):
        greet({"fsdp": lax.rem(f + d, n_fsdp)})
        count += 1
    for d in range(1, n_sp):
        greet({"sp": lax.rem(s + d, n_sp)})
        count += 1
    for stage in tree:
        for d in range(1, stage[1]):
            greet(tree_peer(stage, d))
            count += 1

    @pl.when(has_before)
    def _():
        greet({"span": before})

    @pl.when(has_after)
    def _():
        greet({"span": after})

    count += lax.div(g + n_span - 1, n_span) + lax.div(2 * n_span - 2 - g, n_span)
    pl.semaphore_wait(barrier, count)

    def remote(src, dst, send, recv, device):
        return pltpu.make_async_remote_copy(
            src_ref=src, dst_ref=dst, send_sem=send, recv_sem=recv,
            device_id=device, device_id_type=pl.DeviceIdType.MESH,
        )

    def columns(c):
        return pl.ds(pl.multiple_of(c * chunk_width, HDIM), chunk_width)

    def shifted(base, c):
        return pl.ds(pl.multiple_of(base * width + c * chunk_width, HDIM), chunk_width)

    def row_block(index):
        return pl.ds(pl.multiple_of(index * tokens, tokens), tokens)

    sources = (k_ready, value_ref.at[0], q_ready, grad_ref.at[0])
    homes = (key_joined, value_joined, heads_query, heads_grad)

    def incoming(a, c, d):
        peer = lax.rem(s + d, n_sp)
        return remote(
            sources[a].at[:, shifted(peer, c)], homes[a].at[row_block(s), columns(c)],
            in_s.at[a, c, d - 1], in_r.at[a, c, d - 1], {"sp": peer},
        )

    def incoming_local(a):
        return pltpu.make_async_copy(
            sources[a].at[:, pl.ds(pl.multiple_of(s * width, HDIM), width)],
            homes[a].at[row_block(s), :], in_local.at[a],
        )

    def ahead(a, c):
        home = homes[a]
        return remote(
            home.at[pl.ds(0, group), columns(c)], home.at[pl.ds(group, group), columns(c)],
            ahead_s.at[a, c], ahead_r.at[a, c], {"span": after},
        )

    def behind(a, c):
        return remote(
            (send_key, send_value)[a].at[:, columns(c)],
            (back_key, back_value)[a].at[:, columns(c)],
            behind_s.at[a, c], behind_r.at[a, c], {"span": before},
        )

    results = (dq_heads, dk_heads, dv_heads)
    landed = (dq_rows, dk_rows, dv_rows)

    def outgoing(a, c, d):
        peer = lax.rem(s + d, n_sp)
        return remote(
            results[a].at[row_block(peer), columns(c)], landed[a].at[:, shifted(s, c)],
            out_s.at[a, c, d - 1], out_r.at[a, c, d - 1], {"sp": peer},
        )

    def outgoing_local(a, c):
        return pltpu.make_async_copy(
            results[a].at[row_block(s), columns(c)], landed[a].at[:, shifted(s, c)],
            out_local.at[a, c],
        )

    def gain_copy(d):
        mine = pl.ds(pl.multiple_of(f * part, HDIM), part)
        return remote(
            gain_ref, gain_full.at[:, mine], gain_s.at[d - 1], gain_r.at[d - 1],
            {"fsdp": lax.rem(f + d, n_fsdp)},
        )

    peers = range(1, n_sp)
    for d in range(1, n_fsdp):
        gain_copy(d).start()
    early = min(3, chunks)

    def start_early(a):
        for c in range(early):
            for d in peers:
                incoming(a, c, d).start()
        incoming_local(a).start()

    start_early(1)
    start_early(3)
    gain_full[:, pl.ds(pl.multiple_of(f * part, HDIM), part)] = gain_ref[...]

    @pl.when(g == 0)
    def _():
        key_joined[group:, :] = jnp.zeros((group, width), BF16)
        value_joined[group:, :] = jnp.zeros((group, width), BF16)

    @pl.when(g == n_span - 1)
    def _():
        back_key[...] = jnp.zeros_like(back_key)
        back_value[...] = jnp.zeros_like(back_value)

    for d in range(1, n_fsdp):
        gain_copy(d).wait_recv()

    def norm(raw_ref, row, inverse_ref, ready_ref):
        def block(i, carry):
            rows = pl.ds(pl.multiple_of(i * ROWS, ROWS), ROWS)
            wide = raw_ref[0, rows, :].astype(F32)
            inverse = lax.rsqrt(
                jnp.sum(wide * wide, axis=1, keepdims=True) * (1.0 / channels) + EPSILON
            )
            inverse_ref[rows, :] = inverse
            ready_ref[rows, :] = (wide * inverse * gain_full[row : row + 1, :]).astype(BF16)
            return carry

        lax.fori_loop(0, tokens // ROWS, block, 0)

    norm(key_ref, 1, k_inverse, k_ready)
    start_early(0)
    norm(query_ref, 0, q_inverse, q_ready)
    start_early(2)

    def start_chunk(c, carry):
        for a in range(4):
            for d in peers:
                incoming(a, c, d).start()
        return carry

    lax.fori_loop(early, chunks, start_chunk, 0)

    ids = span_ref[...]
    ids_down = jnp.transpose(jnp.broadcast_to(ids.astype(F32), (HDIM, group)))[:, :1]
    bias[:group, :] = jnp.where(ids_down <= ids.astype(F32), 0.0, NEGATIVE)
    bias[group:, :] = jnp.zeros((group, group), F32) + jnp.where(has_before, 0.0, NEGATIVE)
    weight = jnp.zeros(ids.shape, F32)
    for index in range(steps_ref.shape[1]):
        weight = jnp.where(ids == index, steps_ref[0, index].astype(F32), weight)
    weight_row[...] = weight

    for a in range(4):
        incoming_local(a).wait()

    def forward(c):
        for a in (0, 1):
            for d in peers:
                incoming(a, c, d).wait_recv()

            @pl.when(has_after)
            def _():
                ahead(a, c).start()

    def one_block(head, block_index):
        cols = pl.ds(pl.multiple_of(head * HDIM, HDIM), HDIM)
        if query_block == group:
            rows = pl.ds(0, group)
        else:
            rows = pl.ds(pl.multiple_of(block_index * query_block, query_block), query_block)
        query = heads_query[rows, cols]
        grad = heads_grad[rows, cols]
        keys = key_joined[:, cols]
        scores = dot(keys, query, 1, 1) * (scale * math.log2(math.e)) + bias[:, rows]
        top = jnp.max(scores, axis=0, keepdims=True)
        raised = jnp.exp2(scores - top)
        inverse_total = 1.0 / jnp.sum(raised, axis=0, keepdims=True)
        grad_prob = dot(value_joined[:, cols], grad, 1, 1)
        delta = jnp.sum(raised * grad_prob, axis=0, keepdims=True) * inverse_total
        weighted = raised * (weight_row[:, rows] * inverse_total)
        sgrad = (weighted * (grad_prob - delta)).astype(BF16)
        weights = weighted.astype(BF16)
        dq_heads[rows, cols] = (dot(sgrad, keys, 0, 0) * scale).astype(BF16)
        return dot(sgrad, query, 1, 0) * scale, dot(weights, grad, 1, 0)

    def one_head(head):
        cols = pl.ds(pl.multiple_of(head * HDIM, HDIM), HDIM)
        if query_block == group:
            key_term, value_term = one_block(head, 0)
        else:
            zero = jnp.zeros((2 * group, HDIM), F32)

            def add(i, total):
                terms = one_block(head, i)
                return total[0] + terms[0], total[1] + terms[1]

            key_term, value_term = lax.fori_loop(0, group // query_block, add, (zero, zero))
        own_key[:, cols] = key_term[:group]
        own_value[:, cols] = value_term[:group]
        send_key[:, cols] = key_term[group:].astype(BF16)
        send_value[:, cols] = value_term[group:].astype(BF16)

    def compute(c):
        for a in (2, 3):
            for d in peers:
                incoming(a, c, d).wait_recv()

        @pl.when(has_before)
        def _():
            for a in (0, 1):
                ahead(a, c).wait_recv()

        def head_step(i, carry):
            one_head(c * per_chunk + i)
            return carry

        lax.fori_loop(0, per_chunk, head_step, 0)

        @pl.when(has_before)
        def _():
            for a in (0, 1):
                behind(a, c).start()

        for d in peers:
            outgoing(0, c, d).start()
        outgoing_local(0, c).start()

    def finish(c):
        cols = columns(c)

        @pl.when(has_after)
        def _():
            for a in (0, 1):
                behind(a, c).wait_recv()

        for a, own, back in ((1, own_key, back_key), (2, own_value, back_value)):
            results[a][:, cols] = (own[:, cols] + back[:, cols].astype(F32)).astype(BF16)
            for d in peers:
                outgoing(a, c, d).start()
            outgoing_local(a, c).start()

    lead = min(4, chunks)
    lag = min(4, chunks)
    for c in range(lead):
        forward(c)

    def chunk_step(c, carry):
        @pl.when(c + lead < chunks)
        def _():
            forward(c + lead)

        @pl.when(c < chunks)
        def _():
            compute(c)

        @pl.when(c >= lag)
        def _():
            finish(c - lag)

        return carry

    lax.fori_loop(0, chunks + lag, chunk_step, 0)

    def arrive(a):
        def wait(c, carry):
            for d in peers:
                outgoing(a, c, d).wait_recv()
            outgoing_local(a, c).wait()
            return carry

        lax.fori_loop(0, chunks, wait, 0)

    def norm_backward(raw_ref, row, inverse_ref, rows_ref, out_ref):
        gain_rows[...] = jnp.zeros_like(gain_rows)

        def block(i, carry):
            rows = pl.ds(pl.multiple_of(i * ROWS, ROWS), ROWS)
            inverse = inverse_ref[rows, :]
            normal = raw_ref[0, rows, :].astype(F32) * inverse
            upstream = rows_ref[rows, :].astype(F32)
            scaled = upstream * gain_full[row : row + 1, :]
            inner = jnp.sum(scaled * normal, axis=1, keepdims=True) * (1.0 / channels)
            out_ref[0, rows, :] = (inverse * (scaled - normal * inner)).astype(BF16)
            gain_rows[...] += upstream * normal
            return carry

        lax.fori_loop(0, tokens // ROWS, block, 0)
        gain_part[row : row + 1, :] = jnp.sum(gain_rows[...], axis=0, keepdims=True)

    arrive(0)
    norm_backward(query_ref, 0, q_inverse, dq_rows, query_out)
    arrive(1)
    norm_backward(key_ref, 1, k_inverse, dk_rows, key_out)

    def pair_copy(d):
        peer = lax.rem(f + d, n_fsdp)
        return remote(
            gain_part.at[:, pl.ds(pl.multiple_of(peer * part, HDIM), part)],
            pair_recv.at[d - 1], pair_s.at[d - 1], pair_r.at[d - 1], {"fsdp": peer},
        )

    for d in range(1, n_fsdp):
        pair_copy(d).start()
    arrive(2)
    value_out[0] = dv_rows[...]
    total = gain_part[:, pl.ds(pl.multiple_of(f * part, HDIM), part)]
    for d in range(1, n_fsdp):
        pair_copy(d).wait_recv()
        total = total + pair_recv[d - 1]
    tree_copies = []
    for b, stage in enumerate(tree):
        tree_send[b] = total
        copies = [
            remote(
                tree_send.at[b], tree_recv.at[b, digit(stage)],
                tree_s.at[b, d - 1], tree_r.at[b, d - 1], tree_peer(stage, d),
            )
            for d in range(1, stage[1])
        ]
        for copy in copies:
            copy.start()
        tree_recv[b, digit(stage)] = total
        for copy in copies:
            copy.wait_recv()
        total = tree_recv[b, 0]
        for index in range(1, stage[1]):
            total = total + tree_recv[b, index]
        tree_copies += copies
    gain_out[...] = total

    for copy in tree_copies:
        copy.wait_send()
    for d in range(1, n_fsdp):
        gain_copy(d).wait_send()
        pair_copy(d).wait_send()

    def drain(c, carry):
        for d in peers:
            for a in range(4):
                incoming(a, c, d).wait_send()
            for a in range(3):
                outgoing(a, c, d).wait_send()

        @pl.when(has_after)
        def _():
            for a in (0, 1):
                ahead(a, c).wait_send()

        @pl.when(has_before)
        def _():
            for a in (0, 1):
                behind(a, c).wait_send()

        return carry

    lax.fori_loop(0, chunks, drain, 0)


def on_device(sizes, query_pre, key_pre, values, cotangent, gains, frame_span, denoise_steps):
    n_span, n_sp, n_fsdp = sizes
    _, tokens, channels = query_pre.shape
    group, width, part = tokens * n_sp, channels // n_sp, channels // n_fsdp
    heads = width // HDIM
    per_chunk = 1
    chunks = heads // per_chunk
    stages = stages_of(n_span * n_sp)
    tree = max(1, len(stages))
    most = max([size for _, size in stages] + [2])
    vmem = pltpu.VMEM
    dma = pltpu.SemaphoreType.DMA
    scratch = [
        vmem((2, channels), F32),
        vmem((tokens, channels), BF16), vmem((tokens, channels), BF16),
        vmem((tokens, 1), F32), vmem((tokens, 1), F32),
        vmem((group, width), BF16), vmem((group, width), BF16),
        vmem((2 * group, width), BF16), vmem((2 * group, width), BF16),
        vmem((2 * group, group), F32), vmem((1, group), F32),
        vmem((group, width), F32), vmem((group, width), F32),
        vmem((group, width), BF16), vmem((group, width), BF16),
        vmem((group, width), BF16), vmem((group, width), BF16),
        vmem((group, width), BF16), vmem((group, width), BF16), vmem((group, width), BF16),
        vmem((tokens, channels), BF16), vmem((tokens, channels), BF16),
        vmem((tokens, channels), BF16),
        vmem((2, channels), F32), vmem((ROWS, channels), F32),
        vmem((max(1, n_fsdp - 1), 2, part), F32),
        vmem((tree, 2, part), F32), vmem((tree, most, 2, part), F32),
        dma((max(1, n_fsdp - 1),)), dma((max(1, n_fsdp - 1),)),
        dma((4, chunks, max(1, n_sp - 1))), dma((4, chunks, max(1, n_sp - 1))), dma((4,)),
        dma((2, chunks)), dma((2, chunks)), dma((2, chunks)), dma((2, chunks)),
        dma((3, chunks, max(1, n_sp - 1))), dma((3, chunks, max(1, n_sp - 1))),
        dma((3, chunks)),
        dma((max(1, n_fsdp - 1),)), dma((max(1, n_fsdp - 1),)), dma((tree, most - 1)),
        dma((tree, most - 1)),
    ]
    in_vmem = pl.BlockSpec(memory_space=pltpu.VMEM)
    pairs = heads * group * 2 * group
    return pl.pallas_call(
        functools.partial(kernel, (n_span, n_sp, n_fsdp, chunks, per_chunk)),
        out_shape=(
            jax.ShapeDtypeStruct(query_pre.shape, BF16),
            jax.ShapeDtypeStruct(query_pre.shape, BF16),
            jax.ShapeDtypeStruct(query_pre.shape, BF16),
            jax.ShapeDtypeStruct((2, part), F32),
        ),
        in_specs=[in_vmem] * 6 + [pl.BlockSpec(memory_space=pltpu.SMEM)],
        out_specs=[in_vmem] * 4,
        scratch_shapes=scratch,
        cost_estimate=pl.CostEstimate(
            flops=10 * pairs * HDIM, bytes_accessed=14 * tokens * channels, transcendentals=pairs
        ),
        compiler_params=pltpu.CompilerParams(
            collective_id=0, has_side_effects=True, vmem_limit_bytes=56 * 2**20
        ),
    )(query_pre, key_pre, values, cotangent, gains, frame_span, denoise_steps)


def solution(mesh):
    sizes = (mesh.shape["span"], mesh.shape["sp"], mesh.shape["fsdp"])
    rows = P("fsdp", ("span", "sp"), None)
    return jax.shard_map(
        functools.partial(on_device, sizes),
        mesh=mesh,
        in_specs=(rows, rows, rows, rows, P(None, "fsdp"), P("fsdp", "span"), P("fsdp", None)),
        out_specs=(rows, rows, rows, P(None, "fsdp")),
        check_vma=False,
    )
```
